256 devices in a mesh: group: 16 (over z_hi, y, core), tensor: 16 (over x, z_lo).
Axes of the slice: x: 4, y: 4, z: 8 (z_hi: 2, z_lo: 4; z = z_hi * 4 + z_lo), core: 2. Of those that a mesh axis runs over, the one named last changes fastest.
Arguments:
- queries: bfloat16 [16384, 8192], P('group', 'tensor'), may hold values from -40 to 40
- resp_kv: bfloat16 [16384, 2048], P('group', 'tensor'), may hold values from -6 to 6
- prefix_kv: bfloat16 [4096, 2048], P('group', 'tensor'), may hold values from -6 to 6
- grad_out: bfloat16 [16384, 8192], P('group', 'tensor'), may hold values from -6 to 6
- lengths: int32 [128], P('group'), may hold values from 1 to 128, as said below
- slot_prompt: int32 [128], P('group'), may hold values from 0 to 7, as said below
Outputs:
- grad_queries: bfloat16 [16384, 8192], P('group', 'tensor')
- grad_resp_kv: bfloat16 [16384, 2048], P('group', 'tensor')
- grad_prefix_kv: bfloat16 [4096, 2048], P('group', 'tensor')
The draws below stay inside these ranges and needn't reach their ends.
Inputs may be any that keep to these rules, and one draw needn't show every extreme that they name: `lengths`: each response's length; some response has length 128. `slot_prompt`: each of the 8 prompts is named by exactly 16 responses.
All inputs are finite; a program needn't handle non-finite values.
Results may differ from the reference program's by a relative error of at most 0.01.
Values may be sent and summed in bfloat16 or wider, within the bound.
A program may use at most 64 MiB of HBM per device.

```python
import jax
import jax.numpy as jnp
from jax import lax

HD = 128
RL = 128
PL = 512
HQ = 64
KVH = 8
NP = 8
RESPONSES = 128
ROWS = 16384
PREFIX = 4096


def shared_uniform(key):
    return jax.random.uniform(key, (ROWS, KVH, HD), jnp.float32, -1.0, 1.0)


def draw_queries(key, part):
    key = jax.random.fold_in(key, 3)
    values = jnp.clip(jax.random.normal(key, (ROWS, HQ, HD), jnp.float32), -6.0, 6.0)
    return values.reshape(ROWS, HQ * HD).astype(jnp.bfloat16)


def draw_resp_kv(key, part):
    base = shared_uniform(key)
    key = jax.random.fold_in(key, 5)
    keys = 1.7 * base
    values = jnp.clip(jax.random.normal(key, (ROWS, KVH, HD), jnp.float32), -6.0, 6.0)
    both = jnp.stack([keys, values], axis=2)
    return both.reshape(ROWS, 2 * KVH * HD).astype(jnp.bfloat16)


def draw_lengths(key, part):
    key = jax.random.fold_in(key, 7)
    first, second = jax.random.split(key)
    drawn = jax.random.randint(first, (RESPONSES,), 1, RL + 1, dtype=jnp.int32)
    target = jax.random.randint(second, (), 0, RESPONSES, dtype=jnp.int32)
    return jnp.where(jnp.arange(RESPONSES, dtype=jnp.int32) == target, RL, drawn).astype(jnp.int32)


def draw_slot_prompt(key, part):
    key = jax.random.fold_in(key, 9)
    order = jax.random.permutation(key, RESPONSES)
    return (order // 16).astype(jnp.int32)


def level_of(rng, extent, pieces, least, largest):
    def one(position, shards_of):
        heights = jax.random.uniform(jax.random.fold_in(jax.random.fold_in(rng, 6), position), (shards_of,), jnp.float32, least / len(pieces), largest / len(pieces))
        return jnp.repeat(jnp.exp(heights), extent[position] // shards_of).reshape((-1,) + (1,) * (len(extent) - position - 1))

    factor_of = one(*pieces[0])
    for cut in pieces[1:]:
        factor_of = factor_of * one(*cut)
    return factor_of


def centred(key, extent, width, most, shards=(), kind=jnp.bfloat16):
    factor_of = level_of(key, extent, shards, -0.22, 0.18) if shards else 1.0
    values = jax.random.normal(key, extent, jnp.float32) * width * factor_of
    return jnp.minimum(jnp.maximum(values, -most), most).astype(kind)


def setup_inputs(seed: int = 0) -> dict:
    seeds = jax.random.split(jax.random.key(seed), 7)
    queries = draw_queries(jax.random.fold_in(seeds[6], 71), 0)
    resp_kv = draw_resp_kv(jax.random.fold_in(seeds[6], 71), 0)
    prefix_kv = centred(seeds[2], (PREFIX, 2 * KVH * HD), 1.0, 6.0, ((0, 16), (1, 16)))
    grad_out = centred(seeds[3], (ROWS, HQ * HD), 1.0, 6.0, ((0, 16), (1, 16)))
    lengths = draw_lengths(jax.random.fold_in(seeds[6], 71), 0)
    slot_prompt = draw_slot_prompt(jax.random.fold_in(seeds[6], 71), 0)
    return {"queries": queries, "resp_kv": resp_kv, "prefix_kv": prefix_kv, "grad_out": grad_out, "lengths": lengths, "slot_prompt": slot_prompt}


def reference(queries, resp_kv, prefix_kv, grad_out, lengths, slot_prompt):
    scale = HD ** -0.5
    ratio = HQ // KVH
    qs = queries.reshape(RESPONSES, RL, KVH, ratio, HD)
    kvs = resp_kv.reshape(RESPONSES, RL, KVH, 2, HD)
    pkv = prefix_kv.reshape(NP, PL, KVH, 2, HD)
    gos = grad_out.reshape(RESPONSES, RL, KVH, ratio, HD)
    pos = jnp.arange(RL, dtype=jnp.int32)
    allowed = jnp.concatenate([jnp.ones((RL, PL), dtype=bool), pos[None, :] <= pos[:, None]], axis=1)

    def step(accum, item):
        q_s, kv_s, go_s, length, prompt = item
        pre = lax.dynamic_index_in_dim(pkv, prompt.astype(jnp.int32), 0, keepdims=False)
        keys = jnp.concatenate([pre[:, :, 0], kv_s[:, :, 0]], axis=0).astype(jnp.float32)
        vals = jnp.concatenate([pre[:, :, 1], kv_s[:, :, 1]], axis=0).astype(jnp.float32)
        qf = q_s.astype(jnp.float32)
        scores = jnp.einsum('ikgd,jkd->kgij', qf, keys) * scale
        scores = jnp.where(allowed[None, None], scores, -1e30)
        top = jnp.max(scores, axis=-1, keepdims=True)
        expo = jnp.exp(scores - top)
        probs = expo / jnp.sum(expo, axis=-1, keepdims=True)
        probs_b = probs.astype(jnp.bfloat16).astype(jnp.float32)
        attended = jnp.einsum('kgij,jkd->ikgd', probs_b, vals)
        live = pos < length
        dout = jnp.where(live[:, None, None, None], go_s, jnp.zeros_like(go_s)).astype(jnp.float32)
        delta = jnp.sum(dout * attended, axis=-1)
        dprob = jnp.einsum('ikgd,jkd->kgij', dout, vals)
        dscore = (probs * (dprob - jnp.transpose(delta, (1, 2, 0))[..., None]) * scale)
        dscore = dscore.astype(jnp.bfloat16).astype(jnp.float32)
        dq = jnp.einsum('kgij,jkd->ikgd', dscore, keys).astype(jnp.bfloat16)
        dk = jnp.einsum('kgij,ikgd->jkd', dscore, qf)
        dv = jnp.einsum('kgij,ikgd->jkd', probs_b, dout)
        both = jnp.stack([dk, dv], axis=2)
        index = prompt.astype(jnp.int32)
        current = lax.dynamic_index_in_dim(accum, index, 0, keepdims=False) + both[:PL]
        accum = lax.dynamic_update_index_in_dim(accum, current, index, 0)
        return accum, (dq, both[PL:].astype(jnp.bfloat16))

    start = jnp.zeros((NP, PL, KVH, 2, HD), jnp.float32)
    accum, (dqs, resp_grads) = lax.scan(step, start, (qs, kvs, gos, lengths, slot_prompt))
    grad_queries = dqs.reshape(ROWS, HQ * HD)
    grad_resp_kv = resp_grads.reshape(ROWS, 2 * KVH * HD)
    grad_prefix_kv = accum.astype(jnp.bfloat16).reshape(PREFIX, 2 * KVH * HD)
    return grad_queries, grad_resp_kv, grad_prefix_kv
```

```python
import functools

import jax
import jax.numpy as jnp
from jax import lax
from jax.experimental import pallas as pl
from jax.experimental.pallas import tpu as pltpu
from jax.sharding import PartitionSpec as P

HD = 128
RL = 128
PL = 512
NP = 8
NS = 8
NH = 4
HALF = PL // 2
COLS = NH * RL
SCALE = HD ** (-0.5)
EXP2 = SCALE * 1.4426950408889634
F32 = jnp.float32
BF16 = jnp.bfloat16
MESH = pl.DeviceIdType.MESH
SENDS = 64


def nt(a, b):
    return lax.dot_general(a, b, (((1,), (1,)), ((), ())), preferred_element_type=F32)


def nn(a, b):
    return lax.dot_general(a, b, (((1,), (0,)), ((), ())), preferred_element_type=F32)


def tn(a, b):
    return lax.dot_general(a, b, (((0,), (0,)), ((), ())), preferred_element_type=F32)


def forward_part(q, do, keys, vals, causal):
    scores = nt(keys, q)
    if causal:
        row = lax.broadcasted_iota(jnp.int32, scores.shape, 0)
        col = lax.broadcasted_iota(jnp.int32, scores.shape, 1) % RL
        scores = jnp.where(row <= col, scores, -1e30)
    top = jnp.max(scores, axis=0, keepdims=True)
    expo = jnp.exp2((scores - top) * EXP2)
    dprob = nt(vals, do)
    total = jnp.sum(expo, axis=0, keepdims=True)
    delta = jnp.sum(expo * dprob, axis=0, keepdims=True)
    return expo, dprob, top, total, delta


def kernel(sp_ref, len_ref, q_hbm, do_hbm, resp_hbm, pref_hbm,
           dq_hbm, dr_ref, dp_out,
           own, sib, resp, q_v, do_v, e_ref, dp_ref, ds_ref, st_ref, run,
           rg, rg_send, rg_recv, sib_send, sib_recv, g_ref, y_recv, z_send, z_recv, dq_v, prev_ref, last_ref,
           load_sem, out_sem, send_sem, own_sem, sib_sem, back_sem, y_sem, z_sem, resp_sem, rg_sem):
    group, tensor = lax.axis_index("group"), lax.axis_index("tensor")
    zh, y, c, kv = group // 8, (group // 2) % 4, group % 2, tensor % 2
    pair = tensor + 1 - 2 * kv

    def device(dz, dy, dc, dl):
        g = ((zh + dz) % 2) * 8 + ((y + dy) % 4) * 2 + (c + dc) % 2
        return (g, pair if dl else tensor)

    peers = [(0, 0, 1, 0), (0, 0, 0, 1), (1, 0, 0, 0), (1, 0, 0, 1), (0, 1, 0, 0), (0, 2, 0, 0), (0, 3, 0, 0)]
    flying = []

    def send(src, dst, recv_sem, to):
        copy = pltpu.make_async_remote_copy(
            src, dst, send_sem.at[len(flying)], recv_sem, device_id=device(*to), device_id_type=MESH
        )
        copy.start()
        flying.append(copy)

    def arrived(ref, recv_sem):
        pltpu.make_async_remote_copy(
            ref, ref, send_sem.at[0], recv_sem, device_id=device(0, 0, 1, 0), device_id_type=MESH
        ).wait_recv()

    mine = zh * 4 + y
    loads = [
        pltpu.make_async_copy(pref_hbm, own.at[kv, mine], load_sem.at[8]),
        pltpu.make_async_copy(resp_hbm, resp.at[kv], load_sem.at[9]),
    ]
    for i, (src, dst) in enumerate(((q_hbm, q_v), (do_hbm, do_v))):
        for h in range(NH):
            loads.append(
                pltpu.make_async_copy(
                    src.at[:, :, pl.ds(h * HD, HD)], dst.at[:, pl.ds(h * RL, RL), :], load_sem.at[i * NH + h]
                )
            )
    for copy in loads:
        copy.start()
    barrier = pltpu.get_barrier_semaphore()
    for to in peers:
        pl.semaphore_signal(barrier, inc=1, device_id=device(*to), device_id_type=MESH)
    pl.semaphore_wait(barrier, len(peers))

    def unit(dz, dy, dl):
        return ((kv + dl) % 2, ((zh + dz) % 2) * 4 + (y + dy) % 4)

    def spread(k, p, targets):
        for to in targets:
            send(own.at[k, p], own.at[k, p], own_sem.at[k, p], to)
        send(own.at[k, p], sib.at[k, p], sib_sem.at[k, p], (0, 0, 1, 0))

    loads[0].wait()
    spread(kv, mine, peers[1:])
    for dz, dl in ((0, 1), (1, 1), (1, 0)):
        k, p = unit(dz, 0, dl)
        arrived(own.at[k, p], own_sem.at[k, p])
        spread(k, p, peers[4:])
    loads[1].wait()
    send(resp.at[kv], resp.at[kv], resp_sem.at[0], (0, 0, 0, 1))

    for s in range(NS):
        at = jnp.int32(-1)
        for j in range(s):
            at = jnp.where(sp_ref[j] == sp_ref[s], j, at)
        prev_ref[s] = at
    for p in range(NP):
        at = jnp.int32(-1)
        for j in range(NS):
            at = jnp.where(sp_ref[j] == p, j, at)
        last_ref[p] = at
    for copy in loads[2:]:
        copy.wait()

    @pl.loop(0, NS)
    def _(s):
        row = lax.broadcasted_iota(jnp.int32, (COLS, HD), 0) % RL
        do_v[s] = jnp.where(row < len_ref[s], do_v[s], jnp.zeros((COLS, HD), BF16))

    for dz, dl in ((0, 0), (0, 1), (1, 1), (1, 0)):
        for dy in (1, 3, 2):
            k, p = unit(dz, dy, dl)
            arrived(own.at[k, p], own_sem.at[k, p])
            spread(k, p, ())

    def forward(keys, vals, part):
        n = RL if part == 2 else HALF

        @pl.loop(0, NS)
        def _(s):
            at = s if part == 2 else sp_ref[s]
            expo, dprob, top, total, delta = forward_part(q_v[s], do_v[s], keys[at], vals[at], part == 2)
            e_ref[s, pl.ds(part * HALF, n)] = expo
            dp_ref[s, pl.ds(part * HALF, n)] = dprob
            st_ref[s, pl.ds(part, 1)] = top
            st_ref[s, pl.ds(3 + part, 1)] = total
            st_ref[s, pl.ds(6 + part, 1)] = delta

    forward(own.at[0], own.at[1], 0)
    arrived(resp.at[1 - kv], resp_sem.at[0])
    forward(resp.at[0], resp.at[1], 2)
    for k in range(2):
        for p in range(NP):
            arrived(sib.at[k, p], sib_sem.at[k, p])
    forward(sib.at[0], sib.at[1], 1)

    @pl.loop(0, NS)
    def _(s):
        tops = st_ref[s, pl.ds(0, 3)]
        factor = jnp.exp2((tops - jnp.max(tops, axis=0, keepdims=True)) * EXP2)
        factor = factor / jnp.sum(factor * st_ref[s, pl.ds(3, 3)], axis=0, keepdims=True)
        st_ref[s, pl.ds(0, 3)] = factor
        st_ref[s, pl.ds(3, 1)] = jnp.sum(factor * st_ref[s, pl.ds(6, 3)], axis=0, keepdims=True)

    def backward(s, part):
        rows = pl.ds(part * HALF, RL if part == 2 else HALF)
        prob = e_ref[s, rows] * st_ref[s, pl.ds(part, 1)]
        ds = (prob * (dp_ref[s, rows] - st_ref[s, pl.ds(3, 1)])).astype(BF16)
        ds_ref[s, rows] = ds
        return nn(ds, q_v[s]) * SCALE, nn(prob.astype(BF16), do_v[s])

    @pl.loop(0, NS)
    def _(s):
        for k, grad in enumerate(backward(s, 2)):
            rg[k, s] = grad
            rg_send[k, s] = grad.astype(BF16)

    send(rg_send.at[1 - kv], rg_recv, rg_sem.at[0], (0, 0, 0, 1))

    def prefix_grads(part):
        @pl.loop(0, NS)
        def _(s):
            prev = prev_ref[s]
            at = jnp.maximum(prev, 0)
            for k, grad in enumerate(backward(s, part)):
                run[k, s] = grad + jnp.where(prev >= 0, run[k, at], 0.0)

    def total_of(k, p):
        last = last_ref[p]
        return jnp.where(last >= 0, run[k, jnp.maximum(last, 0)], 0.0)

    prefix_grads(1)
    for k in range(2):
        @pl.loop(0, NP)
        def _(p, k=k):
            sib_send[k, p] = total_of(k, p).astype(BF16)
        send(sib_send.at[k], sib_recv.at[k], back_sem.at[k], (0, 0, 1, 0))
    prefix_grads(0)
    for k in range(2):
        arrived(sib_recv.at[k], back_sem.at[k])

        @pl.loop(0, NP)
        def _(p, k=k):
            g_ref[k, p // 4, p % 4] = (total_of(k, p) + sib_recv[k, p].astype(F32)).astype(BF16)
        for dy in (1, 3, 2):
            send(g_ref.at[k, :, (y + dy) % 4], y_recv.at[dy - 1, k], y_sem.at[dy - 1, k], (0, dy, 0, 0))

    @pl.loop(0, NS)
    def _(s):
        p = sp_ref[s]
        dqt = (
            tn(own[0, p], ds_ref[s, pl.ds(0, HALF)])
            + tn(sib[0, p], ds_ref[s, pl.ds(HALF, HALF)])
            + tn(resp[0, s], ds_ref[s, pl.ds(PL, RL)])
        ) * SCALE
        for h in range(NH):
            dq_v[s, :, pl.ds(h * HD, HD)] = dqt[:, h * RL:(h + 1) * RL].T.astype(BF16)

    dq_out = pltpu.make_async_copy(dq_v, dq_hbm, out_sem.at[0])
    dq_out.start()
    arrived(rg_recv, rg_sem.at[0])

    @pl.loop(0, NS)
    def _(s):
        dr_ref[s] = (rg[kv, s] + rg_recv[s].astype(F32)).astype(BF16)

    def chip_total(k, z):
        total = g_ref[k, z, y].astype(F32)
        for i in range(3):
            total = total + y_recv[i, k, z].astype(F32)
        return total

    for k in range(2):
        for dy in (1, 3, 2):
            arrived(y_recv.at[dy - 1, k], y_sem.at[dy - 1, k])
    for i, (dz, dl) in enumerate(((1, 0), (1, 1), (0, 1))):
        k, z = (kv + dl) % 2, (zh + dz) % 2
        z_send[i] = chip_total(k, z).astype(BF16)
        send(z_send.at[i], z_recv.at[i], z_sem.at[i], (dz, 0, 0, dl))
    total = chip_total(kv, zh)
    for i in (2, 1, 0):
        arrived(z_recv.at[i], z_sem.at[i])
        total = total + z_recv[i].astype(F32)
    dp_out[...] = total.astype(BF16)
    dq_out.wait()
    for copy in flying:
        copy.wait_send()


def shards(queries, resp_kv, prefix_kv, grad_out, lengths, slot_prompt):
    smem = pl.BlockSpec(memory_space=pltpu.SMEM)
    vmem = pl.BlockSpec(memory_space=pltpu.VMEM)
    hbm = pl.BlockSpec(memory_space=pl.ANY)
    dma = pltpu.SemaphoreType.DMA
    dq, dr, dp = pl.pallas_call(
        kernel,
        out_shape=[
            jax.ShapeDtypeStruct((NS, RL, COLS), BF16),
            jax.ShapeDtypeStruct((NS, RL, HD), BF16),
            jax.ShapeDtypeStruct((HALF, HD), BF16),
        ],
        in_specs=[smem, smem, hbm, hbm, hbm, hbm],
        out_specs=[hbm, vmem, vmem],
        scratch_shapes=[
            pltpu.VMEM((2, NP, HALF, HD), BF16),
            pltpu.VMEM((2, NP, HALF, HD), BF16),
            pltpu.VMEM((2, NS, RL, HD), BF16),
            pltpu.VMEM((NS, COLS, HD), BF16),
            pltpu.VMEM((NS, COLS, HD), BF16),
            pltpu.VMEM((NS, PL + RL, COLS), F32),
            pltpu.VMEM((NS, PL + RL, COLS), F32),
            pltpu.VMEM((NS, PL + RL, COLS), BF16),
            pltpu.VMEM((NS, 16, COLS), F32),
            pltpu.VMEM((2, NS, HALF, HD), F32),
            pltpu.VMEM((2, NS, RL, HD), F32),
            pltpu.VMEM((2, NS, RL, HD), BF16),
            pltpu.VMEM((NS, RL, HD), BF16),
            pltpu.VMEM((2, NP, HALF, HD), BF16),
            pltpu.VMEM((2, NP, HALF, HD), BF16),
            pltpu.VMEM((2, 2, 4, HALF, HD), BF16),
            pltpu.VMEM((3, 2, 2, HALF, HD), BF16),
            pltpu.VMEM((3, HALF, HD), BF16),
            pltpu.VMEM((3, HALF, HD), BF16),
            pltpu.VMEM((NS, RL, COLS), BF16),
            pltpu.SMEM((NS,), jnp.int32),
            pltpu.SMEM((NP,), jnp.int32),
            dma((10,)),
            dma((1,)),
            dma((SENDS,)),
            dma((2, NP)),
            dma((2, NP)),
            dma((2,)),
            dma((3, 2)),
            dma((3,)),
            dma((1,)),
            dma((1,)),
        ],
        compiler_params=pltpu.CompilerParams(
            collective_id=0, has_side_effects=True, vmem_limit_bytes=56 * 2**20
        ),
    )(
        slot_prompt,
        lengths,
        queries.reshape(NS, RL, COLS),
        grad_out.reshape(NS, RL, COLS),
        resp_kv.reshape(NS, RL, HD),
        prefix_kv,
    )
    return dq.reshape(NS * RL, COLS), dr.reshape(NS * RL, HD), dp


def solution(mesh):
    spec = P("group", "tensor")
    return jax.shard_map(
        shards,
        mesh=mesh,
        in_specs=(spec, spec, spec, spec, P("group"), P("group")),
        out_specs=(spec, spec, spec),
        check_vma=False,
    )
```

```python
import functools

import jax
import jax.numpy as jnp
from jax import lax
from jax.experimental import pallas as pl
from jax.experimental.pallas import tpu as pltpu
from jax.sharding import PartitionSpec as P

HD = 128
RL = 128
PL = 512
NP = 8
NS = 8
NH = 4
HALF = PL // 2
COLS = NH * RL
SCALE = HD ** (-0.5)
EXP2 = SCALE * 1.4426950408889634
F32 = jnp.float32
BF16 = jnp.bfloat16
MESH = pl.DeviceIdType.MESH
SENDS = 80


def nt(a, b):
    return lax.dot_general(a, b, (((1,), (1,)), ((), ())), preferred_element_type=F32)


def nn(a, b):
    return lax.dot_general(a, b, (((1,), (0,)), ((), ())), preferred_element_type=F32)


def tn(a, b):
    return lax.dot_general(a, b, (((0,), (0,)), ((), ())), preferred_element_type=F32)


def forward_part(q, do, keys, vals, causal):
    scores = nt(keys, q)
    if causal:
        row = lax.broadcasted_iota(jnp.int32, scores.shape, 0)
        col = lax.broadcasted_iota(jnp.int32, scores.shape, 1) % RL
        scores = jnp.where(row <= col, scores, -1e30)
    top = jnp.max(scores, axis=0, keepdims=True)
    expo = jnp.exp2((scores - top) * EXP2)
    dprob = nt(vals, do)
    total = jnp.sum(expo, axis=0, keepdims=True)
    delta = jnp.sum(expo * dprob, axis=0, keepdims=True)
    return expo, dprob, top, total, delta


def kernel(sp_ref, len_ref, q_hbm, do_hbm, resp_hbm, pref_hbm,
           dq_v, dr_ref, dp_out,
           own_a, own_b, sib_a, sib_b, resp, q_v, do_v, e_ref, dp_ref, ds_ref, st_ref, run, own_sum,
           rg, rg_send, rg_recv, sib_send, sib_recv, g_ref, y_recv, z_send, z_recv, prev_ref, last_ref,
           load_sem, send_sem, near_sem, far_sem, sib_sem, back_sem, y_sem, z_sem, resp_sem, rg_sem):
    group, tensor = lax.axis_index("group"), lax.axis_index("tensor")
    zh, y, c, kv = group // 8, (group // 2) % 4, group % 2, tensor % 2
    pair = tensor + 1 - 2 * kv
    owns, sibs = (own_a, own_b), (sib_a, sib_b)

    def device(dz, dy, dc, dl):
        g = ((zh + dz) % 2) * 8 + ((y + dy) % 4) * 2 + (c + dc) % 2
        return (g, pair if dl else tensor)

    sibling, across, high, far = (0, 0, 1, 0), (0, 0, 0, 1), (1, 0, 0, 0), (1, 0, 0, 1)
    ring = ((0, 1, 0, 0), (0, 3, 0, 0), (0, 2, 0, 0))
    peers = (sibling, across, high, far) + ring
    flying = []

    def send(src, dst, recv_sem, to):
        copy = pltpu.make_async_remote_copy(
            src, dst, send_sem.at[len(flying)], recv_sem, device_id=device(*to), device_id_type=MESH
        )
        copy.start()
        flying.append(copy)

    def arrived(ref, recv_sem):
        pltpu.make_async_remote_copy(
            ref, ref, send_sem.at[0], recv_sem, device_id=device(*sibling), device_id_type=MESH
        ).wait_recv()

    mine, there = zh * 4 + y, (1 - zh) * 4 + y
    loads = [pltpu.make_async_copy(pref_hbm.at[pl.ds(i * RL, RL)], owns[i].at[kv, mine], load_sem.at[8 + i]) for i in range(2)]
    loads.append(pltpu.make_async_copy(resp_hbm, resp.at[kv], load_sem.at[10]))
    for i, (src, dst) in enumerate(((q_hbm, q_v), (do_hbm, do_v))):
        for h in range(NH):
            loads.append(
                pltpu.make_async_copy(
                    src.at[:, :, pl.ds(h * HD, HD)], dst.at[:, pl.ds(h * RL, RL), :], load_sem.at[i * NH + h]
                )
            )
    for copy in loads:
        copy.start()
    barrier = pltpu.get_barrier_semaphore()
    for to in peers:
        pl.semaphore_signal(barrier, inc=1, device_id=device(*to), device_id_type=MESH)
    pl.semaphore_wait(barrier, len(peers))

    def near(i, k, p, to):
        unit = owns[i].at[k, p]
        send(unit, unit, near_sem.at[i, k, p], to)

    def wait_near(i, k, p):
        arrived(owns[i].at[k, p], near_sem.at[i, k, p])

    def mirror(i, src, dst, slot):
        send(src, dst, sib_sem.at[i, slot], sibling)

    for i in range(2):
        loads[i].wait()
        for to in (high, far, across):
            near(i, kv, mine, to)
    for i in range(2):
        for to in ring:
            near(i, kv, mine, to)
        mirror(i, owns[i].at[kv, mine], sibs[i].at[kv, mine], 0)
    for i in range(2):
        wait_near(i, 1 - kv, mine)
        for to in ring:
            near(i, 1 - kv, mine, to)
        mirror(i, owns[i].at[1 - kv, mine], sibs[i].at[1 - kv, mine], 1)
    for i in range(2):
        for k in (1 - kv, kv):
            wait_near(i, k, there)
        block = owns[i].at[:, there]
        for to in ring:
            send(block, block, far_sem.at[i, y], to)
        mirror(i, block, sibs[i].at[:, there], 2)
    loads[2].wait()
    send(resp.at[kv], resp.at[kv], resp_sem.at[0], across)

    for s in range(NS):
        at = jnp.int32(-1)
        for j in range(s):
            at = jnp.where(sp_ref[j] == sp_ref[s], j, at)
        prev_ref[s] = at
    for p in range(NP):
        at = jnp.int32(-1)
        for j in range(NS):
            at = jnp.where(sp_ref[j] == p, j, at)
        last_ref[p] = at
    for copy in loads[3:]:
        copy.wait()

    @pl.loop(0, NS)
    def _(s):
        row = lax.broadcasted_iota(jnp.int32, (COLS, HD), 0) % RL
        do_v[s] = jnp.where(row < len_ref[s], do_v[s], jnp.zeros((COLS, HD), BF16))

    def share(i):
        for j in range(3):
            dy = ring[j][1]
            at = (y - dy + 4) % 4
            p, q = zh * 4 + at, (1 - zh) * 4 + at
            wait_near(i, kv, p)
            wait_near(i, 1 - kv, p)
            mirror(i, owns[i].at[:, p], sibs[i].at[:, p], 3 + j)
        for j in range(3):
            dy = ring[j][1]
            at = (y - dy + 4) % 4
            q = (1 - zh) * 4 + at
            arrived(owns[i].at[:, q], far_sem.at[i, at])
            mirror(i, owns[i].at[:, q], sibs[i].at[:, q], 6 + j)

    def shared(i):
        arrived(sibs[i].at[kv, mine], sib_sem.at[i, 0])
        arrived(sibs[i].at[1 - kv, mine], sib_sem.at[i, 1])
        arrived(sibs[i].at[:, there], sib_sem.at[i, 2])
        for j in range(3):
            at = (y - ring[j][1] + 4) % 4
            arrived(sibs[i].at[:, zh * 4 + at], sib_sem.at[i, 3 + j])
            arrived(sibs[i].at[:, (1 - zh) * 4 + at], sib_sem.at[i, 6 + j])

    def block_of(k, part, s):
        if part == 2:
            return resp[k, s]
        p = sp_ref[s]
        return jnp.concatenate([owns[part][k, p], sibs[part][k, p]], axis=0)

    def forward(part):
        n = RL if part == 2 else HALF

        @pl.loop(0, NS, unroll=4)
        def _(s):
            expo, dprob, top, total, delta = forward_part(
                q_v[s], do_v[s], block_of(0, part, s), block_of(1, part, s), part == 2
            )
            e_ref[s, pl.ds(part * HALF, n)] = expo
            dp_ref[s, pl.ds(part * HALF, n)] = dprob
            st_ref[s, pl.ds(part, 1)] = top
            st_ref[s, pl.ds(3 + part, 1)] = total
            st_ref[s, pl.ds(6 + part, 1)] = delta

    arrived(resp.at[1 - kv], resp_sem.at[0])
    forward(2)
    share(0)
    shared(0)
    forward(0)
    share(1)
    shared(1)
    forward(1)

    @pl.loop(0, NS)
    def _(s):
        tops = st_ref[s, pl.ds(0, 3)]
        factor = jnp.exp2((tops - jnp.max(tops, axis=0, keepdims=True)) * EXP2)
        factor = factor / jnp.sum(factor * st_ref[s, pl.ds(3, 3)], axis=0, keepdims=True)
        st_ref[s, pl.ds(0, 3)] = factor
        st_ref[s, pl.ds(3, 1)] = jnp.sum(factor * st_ref[s, pl.ds(6, 3)], axis=0, keepdims=True)

    def backward(s, part):
        rows = pl.ds(part * HALF, RL if part == 2 else HALF)
        prob = e_ref[s, rows] * st_ref[s, pl.ds(part, 1)]
        ds = (prob * (dp_ref[s, rows] - st_ref[s, pl.ds(3, 1)])).astype(BF16)
        ds_ref[s, rows] = ds
        return nn(ds, q_v[s]) * SCALE, nn(prob.astype(BF16), do_v[s])

    def prefix_grads(i):
        @pl.loop(0, NS, unroll=4)
        def _(s):
            prev = prev_ref[s]
            at = jnp.maximum(prev, 0)
            for k, grad in enumerate(backward(s, i)):
                run[k, s] = grad + jnp.where(prev >= 0, run[k, at], 0.0)

        @pl.loop(0, NP)
        def _(p):
            last = last_ref[p]
            at = jnp.maximum(last, 0)
            for k in range(2):
                total = jnp.where(last >= 0, run[k, at], 0.0)
                own_sum[k, p] = total[:RL]
                sib_send[i, k, p] = total[RL:].astype(BF16)
        send(sib_send.at[i], sib_recv.at[i], back_sem.at[i], sibling)

    def reduce_ring(i):
        arrived(sib_recv.at[i], back_sem.at[i])

        @pl.loop(0, NP)
        def _(p):
            for k in range(2):
                g_ref[i, k, p // 4, p % 4] = (own_sum[k, p] + sib_recv[i, k, p].astype(F32)).astype(BF16)
        for j, to in enumerate(ring):
            send(g_ref.at[i, :, :, (y + to[1]) % 4], y_recv.at[i, j], y_sem.at[i, j], to)

    def reduce_high(i):
        for j in range(3):
            arrived(y_recv.at[i, j], y_sem.at[i, j])
        for j, to in enumerate((high, far, across)):
            z_send[i, j] = chip_total(i, (kv + to[3]) % 2, (zh + to[0]) % 2).astype(BF16)
            send(z_send.at[i, j], z_recv.at[i, j], z_sem.at[i, j], to)

    def chip_total(i, k, z):
        total = g_ref[i, k, z, y].astype(F32)
        for j in range(3):
            total = total + y_recv[i, j, k, z].astype(F32)
        return total

    def query_grads(first, count):
        @pl.loop(first, first + count, unroll=4)
        def _(s):
            p = sp_ref[s]
            keys = jnp.concatenate([block_of(0, part, s) for part in range(3)], axis=0)
            dqt = tn(keys, ds_ref[s]) * SCALE
            for h in range(NH):
                dq_v[s, :, pl.ds(h * HD, HD)] = dqt[:, h * RL:(h + 1) * RL].T.astype(BF16)

    prefix_grads(0)

    @pl.loop(0, NS, unroll=4)
    def _(s):
        for k, grad in enumerate(backward(s, 2)):
            rg[k, s] = grad
            rg_send[k, s] = grad.astype(BF16)

    send(rg_send.at[1 - kv], rg_recv, rg_sem.at[0], across)
    reduce_ring(0)
    prefix_grads(1)
    query_grads(0, 4)
    reduce_ring(1)
    query_grads(4, 4)
    arrived(rg_recv, rg_sem.at[0])

    @pl.loop(0, NS)
    def _(s):
        dr_ref[s] = (rg[kv, s] + rg_recv[s].astype(F32)).astype(BF16)

    for i in range(2):
        reduce_high(i)
    for i in range(2):
        total = chip_total(i, kv, zh)
        for j in (2, 1, 0):
            arrived(z_recv.at[i, j], z_sem.at[i, j])
            total = total + z_recv[i, j].astype(F32)
        dp_out[pl.ds(i * RL, RL)] = total.astype(BF16)
    for copy in flying:
        copy.wait_send()


def finish(*refs):
    sem = refs[-1]
    pairs = list(zip(refs[:3], refs[3:6]))
    copies = [pltpu.make_async_copy(src, dst, sem.at[i]) for i, (src, dst) in enumerate(pairs)]
    for copy in copies:
        copy.start()
    for copy in copies:
        copy.wait()


def shards(queries, resp_kv, prefix_kv, grad_out, lengths, slot_prompt):
    smem = pl.BlockSpec(memory_space=pltpu.SMEM)
    vmem = pl.BlockSpec(memory_space=pltpu.VMEM)
    hbm = pl.BlockSpec(memory_space=pltpu.HBM)
    dma = pltpu.SemaphoreType.DMA
    dq, dr, dp = pl.pallas_call(
        kernel,
        out_shape=[
            pltpu.VMEM((NS, RL, COLS), BF16),
            pltpu.VMEM((NS, RL, HD), BF16),
            pltpu.VMEM((HALF, HD), BF16),
        ],
        in_specs=[smem, smem, hbm, hbm, hbm, hbm],
        out_specs=[vmem, vmem, vmem],
        scratch_shapes=[
            pltpu.VMEM((2, NP, RL, HD), BF16),
            pltpu.VMEM((2, NP, RL, HD), BF16),
            pltpu.VMEM((2, NP, RL, HD), BF16),
            pltpu.VMEM((2, NP, RL, HD), BF16),
            pltpu.VMEM((2, NS, RL, HD), BF16),
            pltpu.VMEM((NS, COLS, HD), BF16),
            pltpu.VMEM((NS, COLS, HD), BF16),
            pltpu.VMEM((NS, PL + RL, COLS), F32),
            pltpu.VMEM((NS, PL + RL, COLS), F32),
            pltpu.VMEM((NS, PL + RL, COLS), BF16),
            pltpu.VMEM((NS, 16, COLS), F32),
            pltpu.VMEM((2, NS, HALF, HD), F32),
            pltpu.VMEM((2, NP, RL, HD), F32),
            pltpu.VMEM((2, NS, RL, HD), F32),
            pltpu.VMEM((2, NS, RL, HD), BF16),
            pltpu.VMEM((NS, RL, HD), BF16),
            pltpu.VMEM((2, 2, NP, RL, HD), BF16),
            pltpu.VMEM((2, 2, NP, RL, HD), BF16),
            pltpu.VMEM((2, 2, 2, 4, RL, HD), BF16),
            pltpu.VMEM((2, 3, 2, 2, RL, HD), BF16),
            pltpu.VMEM((2, 3, RL, HD), BF16),
            pltpu.VMEM((2, 3, RL, HD), BF16),
            pltpu.SMEM((NS,), jnp.int32),
            pltpu.SMEM((NP,), jnp.int32),
            dma((11,)),
            dma((SENDS,)),
            dma((2, 2, NP)),
            dma((2, 4)),
            dma((2, 9)),
            dma((2,)),
            dma((2, 3)),
            dma((2, 3)),
            dma((1,)),
            dma((1,)),
        ],
        compiler_params=pltpu.CompilerParams(
            collective_id=0, has_side_effects=True, vmem_limit_bytes=62 * 2**20
        ),
    )(
        slot_prompt,
        lengths,
        queries.reshape(NS, RL, COLS),
        grad_out.reshape(NS, RL, COLS),
        resp_kv.reshape(NS, RL, HD),
        prefix_kv,
    )
    return dq.reshape(NS * RL, COLS), dr.reshape(NS * RL, HD), dp


def solution(mesh):
    spec = P("group", "tensor")
    return jax.shard_map(
        shards,
        mesh=mesh,
        in_specs=(spec, spec, spec, spec, P("group"), P("group")),
        out_specs=(spec, spec, spec),
        check_vma=False,
    )
```

```python
import functools

import jax
import jax.numpy as jnp
from jax import lax
from jax.experimental import pallas as pl
from jax.experimental.pallas import tpu as pltpu
from jax.sharding import PartitionSpec as P

HD = 128
RL = 128
PL = 512
NP = 8
NS = 8
NH = 4
HALF = PL // 2
PARTS = 2
ROWS = HALF // PARTS
WIDE = 2 * ROWS
COLS = NH * RL
SCALE = HD ** (-0.5)
EXP2 = SCALE * 1.4426950408889634
F32 = jnp.float32
BF16 = jnp.bfloat16
MESH = pl.DeviceIdType.MESH
SENDS = 128


def nt(a, b):
    return lax.dot_general(a, b, (((1,), (1,)), ((), ())), preferred_element_type=F32)


def nn(a, b):
    return lax.dot_general(a, b, (((1,), (0,)), ((), ())), preferred_element_type=F32)


def tn(a, b):
    return lax.dot_general(a, b, (((0,), (0,)), ((), ())), preferred_element_type=F32)


def forward_part(q, do, keys, vals, causal):
    scores = nt(keys, q)
    if causal:
        row = lax.broadcasted_iota(jnp.int32, scores.shape, 0)
        col = lax.broadcasted_iota(jnp.int32, scores.shape, 1) % RL
        scores = jnp.where(row <= col, scores, -1e30)
    top = jnp.max(scores, axis=0, keepdims=True)
    expo = jnp.exp2((scores - top) * EXP2)
    dprob = nt(vals, do)
    total = jnp.sum(expo, axis=0, keepdims=True)
    delta = jnp.sum(expo * dprob, axis=0, keepdims=True)
    return expo, dprob, top, total, delta


def kernel(sp_ref, len_ref, q_hbm, do_hbm, resp_hbm, pref_hbm,
           dq_v, dr_ref, dp_out,
           *scratch):
    owns, sibs = scratch[:PARTS], scratch[PARTS:2 * PARTS]
    (resp, q_v, do_v, e_ref, dp_ref, ds_ref, st_ref, run, own_sum,
     rg, rg_send, rg_recv, sib_send, sib_recv, g_ref, y_recv, z_send, z_recv, prev_ref, last_ref,
     load_sem, send_sem, near_sem, far_sem, sib_sem, back_sem, y_sem, z_sem, resp_sem, rg_sem) = scratch[2 * PARTS:]
    group, tensor = lax.axis_index("group"), lax.axis_index("tensor")
    zh, y, c, kv = group // 8, (group // 2) % 4, group % 2, tensor % 2
    pair = tensor + 1 - 2 * kv

    def device(dz, dy, dc, dl):
        g = ((zh + dz) % 2) * 8 + ((y + dy) % 4) * 2 + (c + dc) % 2
        return (g, pair if dl else tensor)

    sibling, across, high, far = (0, 0, 1, 0), (0, 0, 0, 1), (1, 0, 0, 0), (1, 0, 0, 1)
    ring = ((0, 1, 0, 0), (0, 3, 0, 0), (0, 2, 0, 0))
    peers = (sibling, across, high, far) + ring
    flying = []

    def send(src, dst, recv_sem, to):
        copy = pltpu.make_async_remote_copy(
            src, dst, send_sem.at[len(flying)], recv_sem, device_id=device(*to), device_id_type=MESH
        )
        copy.start()
        flying.append(copy)

    def arrived(ref, recv_sem):
        pltpu.make_async_remote_copy(
            ref, ref, send_sem.at[0], recv_sem, device_id=device(*sibling), device_id_type=MESH
        ).wait_recv()

    mine, there = zh * 4 + y, (1 - zh) * 4 + y
    loads = [pltpu.make_async_copy(pref_hbm.at[pl.ds(i * ROWS, ROWS)], owns[i].at[kv, mine], load_sem.at[9 + i]) for i in range(PARTS)]
    loads.append(pltpu.make_async_copy(resp_hbm, resp.at[kv], load_sem.at[8]))
    for i, (src, dst) in enumerate(((q_hbm, q_v), (do_hbm, do_v))):
        for h in range(NH):
            loads.append(
                pltpu.make_async_copy(
                    src.at[:, :, pl.ds(h * HD, HD)], dst.at[:, pl.ds(h * RL, RL), :], load_sem.at[i * NH + h]
                )
            )
    for copy in loads:
        copy.start()
    barrier = pltpu.get_barrier_semaphore()
    for to in peers:
        pl.semaphore_signal(barrier, inc=1, device_id=device(*to), device_id_type=MESH)
    pl.semaphore_wait(barrier, len(peers))

    def near(i, k, p, to):
        unit = owns[i].at[k, p]
        send(unit, unit, near_sem.at[i, k, p], to)

    def wait_near(i, k, p):
        arrived(owns[i].at[k, p], near_sem.at[i, k, p])

    def mirror(i, src, dst, slot):
        send(src, dst, sib_sem.at[i, slot], sibling)

    for i in range(PARTS):
        loads[i].wait()
        for to in (across, far, high):
            near(i, kv, mine, to)
    for i in range(PARTS):
        for to in ring:
            near(i, kv, mine, to)
    for i in range(PARTS):
        wait_near(i, 1 - kv, mine)
        for to in ring:
            near(i, 1 - kv, mine, to)
    for i in range(PARTS):
        for k in (1 - kv, kv):
            wait_near(i, k, there)
        block = owns[i].at[:, there]
        for to in ring:
            send(block, block, far_sem.at[i, y], to)
    loads[PARTS].wait()
    send(resp.at[kv], resp.at[kv], resp_sem.at[0], across)

    for s in range(NS):
        at = jnp.int32(-1)
        for j in range(s):
            at = jnp.where(sp_ref[j] == sp_ref[s], j, at)
        prev_ref[s] = at
    for p in range(NP):
        at = jnp.int32(-1)
        for j in range(NS):
            at = jnp.where(sp_ref[j] == p, j, at)
        last_ref[p] = at
    for copy in loads[PARTS + 1:]:
        copy.wait()

    @pl.loop(0, NS)
    def _(s):
        row = lax.broadcasted_iota(jnp.int32, (COLS, HD), 0) % RL
        do_v[s] = jnp.where(row < len_ref[s], do_v[s], jnp.zeros((COLS, HD), BF16))

    def share(i):
        for j in range(3):
            p = zh * 4 + (y - ring[j][1] + 4) % 4
            wait_near(i, kv, p)
            wait_near(i, 1 - kv, p)
        block = pl.ds(zh * 4, 4)
        mirror(i, owns[i].at[:, block], sibs[i].at[:, block], 0)
        for j in range(3):
            at = (y - ring[j][1] + 4) % 4
            arrived(owns[i].at[:, (1 - zh) * 4 + at], far_sem.at[i, at])
        block = pl.ds(4 - zh * 4, 4)
        mirror(i, owns[i].at[:, block], sibs[i].at[:, block], 1)

    def shared(i):
        for j, first in enumerate((zh * 4, 4 - zh * 4)):
            arrived(sibs[i].at[:, pl.ds(first, 4)], sib_sem.at[i, j])

    def block_of(k, part, s):
        if part == PARTS:
            return resp[k, s]
        p = sp_ref[s]
        return jnp.concatenate([owns[part][k, p], sibs[part][k, p]], axis=0)

    def forward(part):
        n = RL if part == PARTS else WIDE

        @pl.loop(0, NS, unroll=8)
        def _(s):
            expo, dprob, top, total, delta = forward_part(
                q_v[s], do_v[s], block_of(0, part, s), block_of(1, part, s), part == PARTS
            )
            e_ref[s, pl.ds(part * WIDE, n)] = expo
            dp_ref[s, pl.ds(part * WIDE, n)] = dprob
            st_ref[s, pl.ds(part, 1)] = top
            st_ref[s, pl.ds(PARTS + 1 + part, 1)] = total
            st_ref[s, pl.ds(2 * PARTS + 2 + part, 1)] = delta

    share(0)
    shared(0)
    forward(0)
    share(1)
    arrived(resp.at[1 - kv], resp_sem.at[0])
    forward(PARTS)
    shared(1)
    forward(1)

    @pl.loop(0, NS)
    def _(s):
        tops = st_ref[s, pl.ds(0, PARTS + 1)]
        factor = jnp.exp2((tops - jnp.max(tops, axis=0, keepdims=True)) * EXP2)
        factor = factor / jnp.sum(factor * st_ref[s, pl.ds(PARTS + 1, PARTS + 1)], axis=0, keepdims=True)
        st_ref[s, pl.ds(0, PARTS + 1)] = factor
        st_ref[s, pl.ds(PARTS + 1, 1)] = jnp.sum(factor * st_ref[s, pl.ds(2 * PARTS + 2, PARTS + 1)], axis=0, keepdims=True)

    def backward(s, part):
        rows = pl.ds(part * WIDE, RL if part == PARTS else WIDE)
        prob = e_ref[s, rows] * st_ref[s, pl.ds(part, 1)]
        ds = (prob * (dp_ref[s, rows] - st_ref[s, pl.ds(PARTS + 1, 1)])).astype(BF16)
        ds_ref[s, rows] = ds
        return nn(ds, q_v[s]) * SCALE, nn(prob.astype(BF16), do_v[s])

    def prefix_grads(i, middle=None):
        def slot_grads(s):
            prev = prev_ref[s]
            at = jnp.maximum(prev, 0)
            for k, grad in enumerate(backward(s, i)):
                run[k, s] = grad + jnp.where(prev >= 0, run[k, at], 0.0)

        pl.loop(0, NS // 2, unroll=4)(slot_grads)
        if middle is not None:
            reduce_ring(middle)
        pl.loop(NS // 2, NS, unroll=4)(slot_grads)

        @pl.loop(0, NP)
        def _(p):
            last = last_ref[p]
            at = jnp.maximum(last, 0)
            for k in range(2):
                total = jnp.where(last >= 0, run[k, at], 0.0)
                own_sum[i, k, p] = total[:ROWS]
                sib_send[i, k, p] = total[ROWS:].astype(BF16)
        send(sib_send.at[i], sib_recv.at[i], back_sem.at[i], sibling)

    def reduce_ring(i):
        arrived(sib_recv.at[i], back_sem.at[i])
        for side in range(2):
            z = (zh + 1 - side) % 2

            @pl.loop(0, 4)
            def _(p):
                for k in range(2):
                    both = own_sum[i, k, z * 4 + p] + sib_recv[i, k, z * 4 + p].astype(F32)
                    g_ref[i, side, p, k] = both.astype(BF16)
            for j, to in enumerate(ring):
                send(g_ref.at[i, side, (y + to[1]) % 4], y_recv.at[i, side, j], y_sem.at[i, side, j], to)

    def chip_total(i, side, k):
        total = g_ref[i, side, y, k].astype(F32)
        for j in range(3):
            total = total + y_recv[i, side, j, k].astype(F32)
        return total

    def reduce_high(i, side):
        for j in range(3):
            arrived(y_recv.at[i, side, j], y_sem.at[i, side, j])
        for j, to in enumerate((high, far, across)):
            if to[0] != side:
                z_send[i, j] = chip_total(i, side, (kv + to[3]) % 2).astype(BF16)
                send(z_send.at[i, j], z_recv.at[i, j], z_sem.at[i, j], to)

    def query_grads(first, count):
        @pl.loop(first, first + count, unroll=4)
        def _(s):
            p = sp_ref[s]
            keys = jnp.concatenate([block_of(0, part, s) for part in range(PARTS + 1)], axis=0)
            dqt = tn(keys, ds_ref[s]) * SCALE
            for h in range(NH):
                dq_v[s, :, pl.ds(h * HD, HD)] = dqt[:, h * RL:(h + 1) * RL].T.astype(BF16)

    prefix_grads(0)

    @pl.loop(0, NS, unroll=4)
    def _(s):
        for k, grad in enumerate(backward(s, PARTS)):
            rg[k, s] = grad
            rg_send[k, s] = grad.astype(BF16)

    send(rg_send.at[1 - kv], rg_recv, rg_sem.at[0], across)
    for i in range(1, PARTS):
        prefix_grads(i, i - 1)
    query_grads(0, 4)
    reduce_ring(PARTS - 1)
    query_grads(4, 4)
    arrived(rg_recv, rg_sem.at[0])

    @pl.loop(0, NS)
    def _(s):
        dr_ref[s] = (rg[kv, s] + rg_recv[s].astype(F32)).astype(BF16)

    for i in range(PARTS):
        for side in range(2):
            reduce_high(i, side)
    for i in range(PARTS):
        total = chip_total(i, 1, kv)
        for j in (2, 1, 0):
            arrived(z_recv.at[i, j], z_sem.at[i, j])
            total = total + z_recv[i, j].astype(F32)
        dp_out[pl.ds(i * ROWS, ROWS)] = total.astype(BF16)
    for copy in flying:
        copy.wait_send()


def finish(*refs):
    sem = refs[-1]
    pairs = list(zip(refs[:3], refs[3:6]))
    copies = [pltpu.make_async_copy(src, dst, sem.at[i]) for i, (src, dst) in enumerate(pairs)]
    for copy in copies:
        copy.start()
    for copy in copies:
        copy.wait()


def shards(queries, resp_kv, prefix_kv, grad_out, lengths, slot_prompt):
    smem = pl.BlockSpec(memory_space=pltpu.SMEM)
    vmem = pl.BlockSpec(memory_space=pltpu.VMEM)
    hbm = pl.BlockSpec(memory_space=pltpu.HBM)
    dma = pltpu.SemaphoreType.DMA
    dq, dr, dp = pl.pallas_call(
        kernel,
        out_shape=[
            pltpu.VMEM((NS, RL, COLS), BF16),
            pltpu.VMEM((NS, RL, HD), BF16),
            pltpu.VMEM((HALF, HD), BF16),
        ],
        in_specs=[smem, smem, hbm, hbm, hbm, hbm],
        out_specs=[vmem, vmem, vmem],
        scratch_shapes=[pltpu.VMEM((2, NP, ROWS, HD), BF16)] * (2 * PARTS) + [
            pltpu.VMEM((2, NS, RL, HD), BF16),
            pltpu.VMEM((NS, COLS, HD), BF16),
            pltpu.VMEM((NS, COLS, HD), BF16),
            pltpu.VMEM((NS, PL + RL, COLS), F32),
            pltpu.VMEM((NS, PL + RL, COLS), F32),
            pltpu.VMEM((NS, PL + RL, COLS), BF16),
            pltpu.VMEM((NS, 16, COLS), F32),
            pltpu.VMEM((2, NS, WIDE, HD), F32),
            pltpu.VMEM((PARTS, 2, NP, ROWS, HD), F32),
            pltpu.VMEM((2, NS, RL, HD), F32),
            pltpu.VMEM((2, NS, RL, HD), BF16),
            pltpu.VMEM((NS, RL, HD), BF16),
            pltpu.VMEM((PARTS, 2, NP, ROWS, HD), BF16),
            pltpu.VMEM((PARTS, 2, NP, ROWS, HD), BF16),
            pltpu.VMEM((PARTS, 2, 4, 2, ROWS, HD), BF16),
            pltpu.VMEM((PARTS, 2, 3, 2, ROWS, HD), BF16),
            pltpu.VMEM((PARTS, 3, ROWS, HD), BF16),
            pltpu.VMEM((PARTS, 3, ROWS, HD), BF16),
            pltpu.SMEM((NS,), jnp.int32),
            pltpu.SMEM((NP,), jnp.int32),
            dma((9 + PARTS,)),
            dma((SENDS,)),
            dma((PARTS, 2, NP)),
            dma((PARTS, 4)),
            dma((PARTS, 2)),
            dma((PARTS,)),
            dma((PARTS, 2, 3)),
            dma((PARTS, 3)),
            dma((1,)),
            dma((1,)),
        ],
        compiler_params=pltpu.CompilerParams(
            collective_id=0, has_side_effects=True, vmem_limit_bytes=62 * 2**20
        ),
    )(
        slot_prompt,
        lengths,
        queries.reshape(NS, RL, COLS),
        grad_out.reshape(NS, RL, COLS),
        resp_kv.reshape(NS, RL, HD),
        prefix_kv,
    )
    return dq.reshape(NS * RL, COLS), dr.reshape(NS * RL, HD), dp


def solution(mesh):
    spec = P("group", "tensor")
    return jax.shard_map(
        shards,
        mesh=mesh,
        in_specs=(spec, spec, spec, spec, P("group"), P("group")),
        out_specs=(spec, spec, spec),
        check_vma=False,
    )
```

```python
import functools

import jax
import jax.numpy as jnp
from jax import lax
from jax.experimental import pallas as pl
from jax.experimental.pallas import tpu as pltpu
from jax.sharding import PartitionSpec as P

HD = 128
RL = 128
PL = 512
NP = 8
NS = 8
NH = 4
HALF = PL // 2
PARTS = 2
ROWS = HALF // PARTS
WIDE = 2 * ROWS
COLS = NH * RL
SCALE = HD ** (-0.5)
EXP2 = SCALE * 1.4426950408889634
F32 = jnp.float32
BF16 = jnp.bfloat16
MESH = pl.DeviceIdType.MESH
SENDS = 64
UNROLL = 8


def nt(a, b):
    return lax.dot_general(a, b, (((1,), (1,)), ((), ())), preferred_element_type=F32)


def nn(a, b):
    return lax.dot_general(a, b, (((1,), (0,)), ((), ())), preferred_element_type=F32)


def tn(a, b):
    return lax.dot_general(a, b, (((0,), (0,)), ((), ())), preferred_element_type=F32)


def forward_part(q, do, keys, vals, causal):
    scores = nt(keys, q)
    if causal:
        row = lax.broadcasted_iota(jnp.int32, scores.shape, 0)
        col = lax.broadcasted_iota(jnp.int32, scores.shape, 1) % RL
        scores = jnp.where(row <= col, scores, -1e30)
    top = jnp.max(scores, axis=0, keepdims=True)
    expo = jnp.exp2((scores - top) * EXP2)
    dprob = nt(vals, do)
    total = jnp.sum(expo, axis=0, keepdims=True)
    delta = jnp.sum(expo * dprob, axis=0, keepdims=True)
    return expo, dprob, top, total, delta


def kernel(sp_hbm, len_hbm, q_hbm, do_hbm, resp_hbm, pref_hbm,
           dq_v, dr_ref, dp_out,
           *scratch):
    owns, sibs = scratch[:PARTS], scratch[PARTS:2 * PARTS]
    (resp, q_v, do_v, e_ref, dp_ref, ds_ref, st_ref, run, own_sum,
     rg, rg_send, rg_recv, sib_send, sib_recv, g_ref, y_recv, z_send, z_recv, sp_ref, len_ref, prev_ref, last_ref,
     load_sem, send_sem, near_sem, far_sem, sib_sem, back_sem, y_sem, z_sem, resp_sem, rg_sem) = scratch[2 * PARTS:]
    group, tensor = lax.axis_index("group"), lax.axis_index("tensor")
    zh, y, c, kv = group // 8, (group // 2) % 4, group % 2, tensor % 2
    pair = tensor + 1 - 2 * kv

    def device(dz, dy, dc, dl):
        g = ((zh + dz) % 2) * 8 + ((y + dy) % 4) * 2 + (c + dc) % 2
        return (g, pair if dl else tensor)

    sibling, across, high, far = (0, 0, 1, 0), (0, 0, 0, 1), (1, 0, 0, 0), (1, 0, 0, 1)
    ring = ((0, 1, 0, 0), (0, 3, 0, 0), (0, 2, 0, 0))
    peers = (sibling, across, high, far) + ring
    flying = []

    def send(src, dst, recv_sem, to):
        copy = pltpu.make_async_remote_copy(
            src, dst, send_sem.at[len(flying)], recv_sem, device_id=device(*to), device_id_type=MESH
        )
        copy.start()
        flying.append(copy)

    def arrived(ref, recv_sem):
        pltpu.make_async_remote_copy(
            ref, ref, send_sem.at[0], recv_sem, device_id=device(*sibling), device_id_type=MESH
        ).wait_recv()

    barrier = pltpu.get_barrier_semaphore()
    for to in peers:
        pl.semaphore_signal(barrier, inc=1, device_id=device(*to), device_id_type=MESH)
    mine, there = zh * 4 + y, (1 - zh) * 4 + y
    loads = [pltpu.make_async_copy(pref_hbm.at[pl.ds(i * ROWS, ROWS)], owns[i].at[kv, mine], load_sem.at[9 + i]) for i in range(PARTS)]
    loads.append(pltpu.make_async_copy(resp_hbm, resp.at[kv], load_sem.at[8]))
    for i, (src, dst) in enumerate(((sp_hbm, sp_ref), (len_hbm, len_ref))):
        loads.append(pltpu.make_async_copy(src, dst, load_sem.at[9 + PARTS + i]))
    for i, (src, dst) in enumerate(((q_hbm, q_v), (do_hbm, do_v))):
        for h in range(NH):
            loads.append(
                pltpu.make_async_copy(
                    src.at[:, :, pl.ds(h * HD, HD)], dst.at[:, pl.ds(h * RL, RL), :], load_sem.at[i * NH + h]
                )
            )
    for copy in loads:
        copy.start()
    pl.semaphore_wait(barrier, len(peers))

    def near(i, k, p, to):
        unit = owns[i].at[k, p]
        send(unit, unit, near_sem.at[i, k, p], to)

    def wait_near(i, k, p):
        arrived(owns[i].at[k, p], near_sem.at[i, k, p])

    def mirror(i, src, dst, slot):
        send(src, dst, sib_sem.at[i, slot], sibling)

    for i in range(PARTS):
        loads[i].wait()
        for to in (across, far, high):
            near(i, kv, mine, to)
    for i in range(PARTS):
        for to in ring:
            near(i, kv, mine, to)
    for i in range(PARTS):
        wait_near(i, 1 - kv, mine)
        for to in ring:
            near(i, 1 - kv, mine, to)
    for i in range(PARTS):
        for k in (1 - kv, kv):
            wait_near(i, k, there)
        block = owns[i].at[:, there]
        for to in ring:
            send(block, block, far_sem.at[i, y], to)
    loads[PARTS].wait()
    send(resp.at[kv], resp.at[kv], resp_sem.at[0], across)

    for copy in loads[PARTS + 1:]:
        copy.wait()
    for s in range(NS):
        at = jnp.int32(-1)
        for j in range(s):
            at = jnp.where(sp_ref[j] == sp_ref[s], j, at)
        prev_ref[s] = at
    for p in range(NP):
        at = jnp.int32(-1)
        for j in range(NS):
            at = jnp.where(sp_ref[j] == p, j, at)
        last_ref[p] = at

    @pl.loop(0, NS)
    def _(s):
        row = lax.broadcasted_iota(jnp.int32, (COLS, HD), 0) % RL
        do_v[s] = jnp.where(row < len_ref[s], do_v[s], jnp.zeros((COLS, HD), BF16))

    def share(i):
        for j in range(3):
            p = zh * 4 + (y - ring[j][1] + 4) % 4
            wait_near(i, kv, p)
            wait_near(i, 1 - kv, p)
        block = pl.ds(zh * 4, 4)
        mirror(i, owns[i].at[:, block], sibs[i].at[:, block], 0)
        for j in range(3):
            at = (y - ring[j][1] + 4) % 4
            arrived(owns[i].at[:, (1 - zh) * 4 + at], far_sem.at[i, at])
        block = pl.ds(4 - zh * 4, 4)
        mirror(i, owns[i].at[:, block], sibs[i].at[:, block], 1)

    def shared(i):
        for j, first in enumerate((zh * 4, 4 - zh * 4)):
            arrived(sibs[i].at[:, pl.ds(first, 4)], sib_sem.at[i, j])

    def block_of(k, part, s):
        if part == PARTS:
            return resp[k, s]
        p = sp_ref[s]
        return jnp.concatenate([owns[part][k, p], sibs[part][k, p]], axis=0)

    def forward(part):
        n = RL if part == PARTS else WIDE

        @pl.loop(0, NS, unroll=8)
        def _(s):
            expo, dprob, top, total, delta = forward_part(
                q_v[s], do_v[s], block_of(0, part, s), block_of(1, part, s), part == PARTS
            )
            e_ref[s, pl.ds(part * WIDE, n)] = expo
            dp_ref[s, pl.ds(part * WIDE, n)] = dprob
            st_ref[s, pl.ds(part, 1)] = top
            st_ref[s, pl.ds(PARTS + 1 + part, 1)] = total
            st_ref[s, pl.ds(2 * PARTS + 2 + part, 1)] = delta

    share(0)
    shared(0)
    forward(0)
    share(1)
    arrived(resp.at[1 - kv], resp_sem.at[0])
    forward(PARTS)
    shared(1)
    forward(1)

    @pl.loop(0, NS)
    def _(s):
        tops = st_ref[s, pl.ds(0, PARTS + 1)]
        factor = jnp.exp2((tops - jnp.max(tops, axis=0, keepdims=True)) * EXP2)
        factor = factor / jnp.sum(factor * st_ref[s, pl.ds(PARTS + 1, PARTS + 1)], axis=0, keepdims=True)
        st_ref[s, pl.ds(0, PARTS + 1)] = factor
        st_ref[s, pl.ds(PARTS + 1, 1)] = jnp.sum(factor * st_ref[s, pl.ds(2 * PARTS + 2, PARTS + 1)], axis=0, keepdims=True)

    def backward(s, part, first, n):
        rows = pl.ds(part * WIDE + first, n)
        prob = e_ref[s, rows] * st_ref[s, pl.ds(part, 1)]
        ds = (prob * (dp_ref[s, rows] - st_ref[s, pl.ds(PARTS + 1, 1)])).astype(BF16)
        ds_ref[s, rows] = ds
        return nn(ds, q_v[s]) * SCALE, nn(prob.astype(BF16), do_v[s])

    def prefix_grads(i, first, save):
        @pl.loop(0, NS, unroll=UNROLL)
        def _(s):
            prev = prev_ref[s]
            at = jnp.maximum(prev, 0)
            for k, grad in enumerate(backward(s, i, first, ROWS)):
                run[k, s] = grad + jnp.where(prev >= 0, run[k, at], 0.0)

        @pl.loop(0, NP)
        def _(p):
            last = last_ref[p]
            at = jnp.maximum(last, 0)
            for k in range(2):
                save(k, p, jnp.where(last >= 0, run[k, at], 0.0))

    def sibling_grads(i):
        def save(k, p, total):
            sib_send[i, k, p] = total.astype(BF16)

        prefix_grads(i, ROWS, save)
        send(sib_send.at[i], sib_recv.at[i], back_sem.at[i], sibling)

    def own_grads(i):
        def save(k, p, total):
            own_sum[i, k, p] = total

        prefix_grads(i, 0, save)

    def reduce_ring(i):
        arrived(sib_recv.at[i], back_sem.at[i])
        for side in range(2):
            z = (zh + 1 - side) % 2

            @pl.loop(0, 4)
            def _(p):
                for k in range(2):
                    both = own_sum[i, k, z * 4 + p] + sib_recv[i, k, z * 4 + p].astype(F32)
                    g_ref[i, side, p, k] = both.astype(BF16)
            for j, to in enumerate(ring):
                send(g_ref.at[i, side, (y + to[1]) % 4], y_recv.at[i, side, j], y_sem.at[i, side, j], to)

    def chip_total(i, side, k):
        total = g_ref[i, side, y, k].astype(F32)
        for j in range(3):
            total = total + y_recv[i, side, j, k].astype(F32)
        return total

    def reduce_high(i, side):
        for j in range(3):
            arrived(y_recv.at[i, side, j], y_sem.at[i, side, j])
        for j, to in enumerate((high, far, across)):
            if to[0] != side:
                z_send[i, j] = chip_total(i, side, (kv + to[3]) % 2).astype(BF16)
                send(z_send.at[i, j], z_recv.at[i, j], z_sem.at[i, j], to)

    def query_grads(first, count):
        @pl.loop(first, first + count, unroll=4)
        def _(s):
            p = sp_ref[s]
            keys = jnp.concatenate([block_of(0, part, s) for part in range(PARTS + 1)], axis=0)
            dqt = tn(keys, ds_ref[s]) * SCALE
            for h in range(NH):
                dq_v[s, :, pl.ds(h * HD, HD)] = dqt[:, h * RL:(h + 1) * RL].T.astype(BF16)

    sibling_grads(0)
    own_grads(0)
    reduce_ring(0)

    @pl.loop(0, NS, unroll=4)
    def _(s):
        for k, grad in enumerate(backward(s, PARTS, 0, RL)):
            rg[k, s] = grad
            rg_send[k, s] = grad.astype(BF16)

    send(rg_send.at[1 - kv], rg_recv, rg_sem.at[0], across)
    sibling_grads(1)
    own_grads(1)
    query_grads(0, 4)
    reduce_ring(1)
    query_grads(4, 4)
    reduce_high(0, 0)
    reduce_high(0, 1)
    arrived(rg_recv, rg_sem.at[0])

    @pl.loop(0, NS)
    def _(s):
        dr_ref[s] = (rg[kv, s] + rg_recv[s].astype(F32)).astype(BF16)

    reduce_high(1, 0)
    reduce_high(1, 1)
    for i in range(PARTS):
        total = chip_total(i, 1, kv)
        for j in (2, 1, 0):
            arrived(z_recv.at[i, j], z_sem.at[i, j])
            total = total + z_recv[i, j].astype(F32)
        dp_out[pl.ds(i * ROWS, ROWS)] = total.astype(BF16)
    for copy in flying:
        copy.wait_send()


def finish(*refs):
    sem = refs[-1]
    pairs = list(zip(refs[:3], refs[3:6]))
    copies = [pltpu.make_async_copy(src, dst, sem.at[i]) for i, (src, dst) in enumerate(pairs)]
    for copy in copies:
        copy.start()
    for copy in copies:
        copy.wait()


def shards(queries, resp_kv, prefix_kv, grad_out, lengths, slot_prompt):
    vmem = pl.BlockSpec(memory_space=pltpu.VMEM)
    hbm = pl.BlockSpec(memory_space=pltpu.HBM)
    dma = pltpu.SemaphoreType.DMA
    dq, dr, dp = pl.pallas_call(
        kernel,
        out_shape=[
            pltpu.VMEM((NS, RL, COLS), BF16),
            pltpu.VMEM((NS, RL, HD), BF16),
            pltpu.VMEM((HALF, HD), BF16),
        ],
        in_specs=[hbm, hbm, hbm, hbm, hbm, hbm],
        out_specs=[vmem, vmem, vmem],
        scratch_shapes=[pltpu.VMEM((2, NP, ROWS, HD), BF16)] * (2 * PARTS) + [
            pltpu.VMEM((2, NS, RL, HD), BF16),
            pltpu.VMEM((NS, COLS, HD), BF16),
            pltpu.VMEM((NS, COLS, HD), BF16),
            pltpu.VMEM((NS, PL + RL, COLS), F32),
            pltpu.VMEM((NS, PL + RL, COLS), F32),
            pltpu.VMEM((NS, PL + RL, COLS), BF16),
            pltpu.VMEM((NS, 16, COLS), F32),
            pltpu.VMEM((2, NS, ROWS, HD), F32),
            pltpu.VMEM((PARTS, 2, NP, ROWS, HD), F32),
            pltpu.VMEM((2, NS, RL, HD), F32),
            pltpu.VMEM((2, NS, RL, HD), BF16),
            pltpu.VMEM((NS, RL, HD), BF16),
            pltpu.VMEM((PARTS, 2, NP, ROWS, HD), BF16),
            pltpu.VMEM((PARTS, 2, NP, ROWS, HD), BF16),
            pltpu.VMEM((PARTS, 2, 4, 2, ROWS, HD), BF16),
            pltpu.VMEM((PARTS, 2, 3, 2, ROWS, HD), BF16),
            pltpu.VMEM((PARTS, 3, ROWS, HD), BF16),
            pltpu.VMEM((PARTS, 3, ROWS, HD), BF16),
            pltpu.SMEM((NS,), jnp.int32),
            pltpu.SMEM((NS,), jnp.int32),
            pltpu.SMEM((NS,), jnp.int32),
            pltpu.SMEM((NP,), jnp.int32),
            dma((11 + PARTS,)),
            dma((SENDS,)),
            dma((PARTS, 2, NP)),
            dma((PARTS, 4)),
            dma((PARTS, 2)),
            dma((PARTS,)),
            dma((PARTS, 2, 3)),
            dma((PARTS, 3)),
            dma((1,)),
            dma((1,)),
        ],
        compiler_params=pltpu.CompilerParams(
            collective_id=0, has_side_effects=True, vmem_limit_bytes=62 * 2**20
        ),
    )(
        slot_prompt,
        lengths,
        queries.reshape(NS, RL, COLS),
        grad_out.reshape(NS, RL, COLS),
        resp_kv.reshape(NS, RL, HD),
        prefix_kv,
    )
    return dq.reshape(NS * RL, COLS), dr.reshape(NS * RL, HD), dp


def solution(mesh):
    spec = P("group", "tensor")
    return jax.shard_map(
        shards,
        mesh=mesh,
        in_specs=(spec, spec, spec, spec, P("group"), P("group")),
        out_specs=(spec, spec, spec),
        check_vma=False,
    )
```

```python
import functools

import jax
import jax.numpy as jnp
from jax import lax
from jax.experimental import pallas as pl
from jax.experimental.pallas import tpu as pltpu
from jax.sharding import PartitionSpec as P

HD = 128
RL = 128
PL = 512
NP = 8
NS = 8
NH = 4
HALF = PL // 2
PARTS = 2
ROWS = HALF // PARTS
WIDE = 2 * ROWS
COLS = NH * RL
SCALE = HD ** (-0.5)
EXP2 = SCALE * 1.4426950408889634
F32 = jnp.float32
BF16 = jnp.bfloat16
MESH = pl.DeviceIdType.MESH
SENDS = 64
UNROLL = 8


def nt(a, b):
    return lax.dot_general(a, b, (((1,), (1,)), ((), ())), preferred_element_type=F32)


def nn(a, b):
    return lax.dot_general(a, b, (((1,), (0,)), ((), ())), preferred_element_type=F32)


def tn(a, b):
    return lax.dot_general(a, b, (((0,), (0,)), ((), ())), preferred_element_type=F32)


def forward_part(q, do, keys, vals, causal):
    scores = nt(keys, q)
    if causal:
        row = lax.broadcasted_iota(jnp.int32, scores.shape, 0)
        col = lax.broadcasted_iota(jnp.int32, scores.shape, 1) % RL
        scores = jnp.where(row <= col, scores, -1e30)
    top = jnp.max(scores, axis=0, keepdims=True)
    expo = jnp.exp2((scores - top) * EXP2)
    dprob = nt(vals, do)
    total = jnp.sum(expo, axis=0, keepdims=True)
    delta = jnp.sum(expo * dprob, axis=0, keepdims=True)
    return expo, dprob, top, total, delta


def kernel(sp_hbm, len_hbm, q_hbm, do_hbm, resp_hbm, pref_hbm,
           dq_v, dr_ref, dp_out,
           *scratch):
    owns, sibs = scratch[:PARTS], scratch[PARTS:2 * PARTS]
    (resp, q_v, do_v, e_ref, dp_ref, ds_ref, st_ref, run, own_sum,
     rg, rg_send, rg_recv, sib_send, sib_recv, g_ref, y_recv, z_send, z_recv, sp_ref, len_ref, prev_ref, last_ref,
     load_sem, send_sem, near_sem, far_sem, sib_sem, back_sem, y_sem, z_sem, resp_sem, rg_sem) = scratch[2 * PARTS:]
    group, tensor = lax.axis_index("group"), lax.axis_index("tensor")
    zh, y, c, kv = group // 8, (group // 2) % 4, group % 2, tensor % 2
    pair = tensor + 1 - 2 * kv

    def device(dz, dy, dc, dl):
        g = ((zh + dz) % 2) * 8 + ((y + dy) % 4) * 2 + (c + dc) % 2
        return (g, pair if dl else tensor)

    sibling, across, high, far = (0, 0, 1, 0), (0, 0, 0, 1), (1, 0, 0, 0), (1, 0, 0, 1)
    ring = ((0, 2, 0, 0), (0, 1, 0, 0), (0, 3, 0, 0))
    peers = (sibling, across, high, far) + ring
    flying = []

    def send(src, dst, recv_sem, to):
        copy = pltpu.make_async_remote_copy(
            src, dst, send_sem.at[len(flying)], recv_sem, device_id=device(*to), device_id_type=MESH
        )
        copy.start()
        flying.append(copy)

    def arrived(ref, recv_sem):
        pltpu.make_async_remote_copy(
            ref, ref, send_sem.at[0], recv_sem, device_id=device(*sibling), device_id_type=MESH
        ).wait_recv()

    barrier = pltpu.get_barrier_semaphore()
    for to in peers:
        pl.semaphore_signal(barrier, inc=1, device_id=device(*to), device_id_type=MESH)
    mine, there = zh * 4 + y, (1 - zh) * 4 + y
    loads = [pltpu.make_async_copy(pref_hbm.at[pl.ds(i * ROWS, ROWS)], owns[i].at[kv, mine], load_sem.at[9 + i]) for i in range(PARTS)]
    loads.append(pltpu.make_async_copy(resp_hbm, resp.at[kv], load_sem.at[8]))
    for i, (src, dst) in enumerate(((sp_hbm, sp_ref), (len_hbm, len_ref))):
        loads.append(pltpu.make_async_copy(src, dst, load_sem.at[9 + PARTS + i]))
    for i, (src, dst) in enumerate(((q_hbm, q_v), (do_hbm, do_v))):
        for h in range(NH):
            loads.append(
                pltpu.make_async_copy(
                    src.at[:, :, pl.ds(h * HD, HD)], dst.at[:, pl.ds(h * RL, RL), :], load_sem.at[i * NH + h]
                )
            )
    for copy in loads:
        copy.start()
    pl.semaphore_wait(barrier, len(peers))

    def near(i, k, p, to):
        unit = owns[i].at[k, p]
        send(unit, unit, near_sem.at[i, k, p], to)

    def wait_near(i, k, p):
        arrived(owns[i].at[k, p], near_sem.at[i, k, p])

    def mirror(i, src, dst, slot):
        send(src, dst, sib_sem.at[i, slot], sibling)

    for i in range(PARTS):
        loads[i].wait()
        for to in (across, far, high):
            near(i, kv, mine, to)
    for i in range(PARTS):
        for to in ring:
            near(i, kv, mine, to)
    for i in range(PARTS):
        wait_near(i, 1 - kv, mine)
        for to in ring:
            near(i, 1 - kv, mine, to)
    for i in range(PARTS):
        for k in (1 - kv, kv):
            wait_near(i, k, there)
        block = owns[i].at[:, there]
        for to in ring:
            send(block, block, far_sem.at[i, y], to)
    loads[PARTS].wait()
    send(resp.at[kv], resp.at[kv], resp_sem.at[0], across)

    for copy in loads[PARTS + 1:]:
        copy.wait()
    for s in range(NS):
        at = jnp.int32(-1)
        for j in range(s):
            at = jnp.where(sp_ref[j] == sp_ref[s], j, at)
        prev_ref[s] = at
    for p in range(NP):
        at = jnp.int32(-1)
        for j in range(NS):
            at = jnp.where(sp_ref[j] == p, j, at)
        last_ref[p] = at

    @pl.loop(0, NS)
    def _(s):
        row = lax.broadcasted_iota(jnp.int32, (COLS, HD), 0) % RL
        do_v[s] = jnp.where(row < len_ref[s], do_v[s], jnp.zeros((COLS, HD), BF16))

    def share(i):
        for j in range(3):
            p = zh * 4 + (y - ring[j][1] + 4) % 4
            wait_near(i, kv, p)
            wait_near(i, 1 - kv, p)
        block = pl.ds(zh * 4, 4)
        mirror(i, owns[i].at[:, block], sibs[i].at[:, block], 0)
        for j in range(3):
            at = (y - ring[j][1] + 4) % 4
            arrived(owns[i].at[:, (1 - zh) * 4 + at], far_sem.at[i, at])
        block = pl.ds(4 - zh * 4, 4)
        mirror(i, owns[i].at[:, block], sibs[i].at[:, block], 1)

    def shared(i):
        for j, first in enumerate((zh * 4, 4 - zh * 4)):
            arrived(sibs[i].at[:, pl.ds(first, 4)], sib_sem.at[i, j])

    def block_of(k, part, s):
        if part == PARTS:
            return resp[k, s]
        p = sp_ref[s]
        return jnp.concatenate([owns[part][k, p], sibs[part][k, p]], axis=0)

    def forward(part):
        n = RL if part == PARTS else WIDE

        @pl.loop(0, NS, unroll=8)
        def _(s):
            expo, dprob, top, total, delta = forward_part(
                q_v[s], do_v[s], block_of(0, part, s), block_of(1, part, s), part == PARTS
            )
            e_ref[s, pl.ds(part * WIDE, n)] = expo
            dp_ref[s, pl.ds(part * WIDE, n)] = dprob
            st_ref[s, pl.ds(part, 1)] = top
            st_ref[s, pl.ds(PARTS + 1 + part, 1)] = total
            st_ref[s, pl.ds(2 * PARTS + 2 + part, 1)] = delta

    share(0)
    shared(0)
    forward(0)
    share(1)
    arrived(resp.at[1 - kv], resp_sem.at[0])
    forward(PARTS)
    shared(1)
    forward(1)

    @pl.loop(0, NS)
    def _(s):
        tops = st_ref[s, pl.ds(0, PARTS + 1)]
        factor = jnp.exp2((tops - jnp.max(tops, axis=0, keepdims=True)) * EXP2)
        factor = factor / jnp.sum(factor * st_ref[s, pl.ds(PARTS + 1, PARTS + 1)], axis=0, keepdims=True)
        st_ref[s, pl.ds(0, PARTS + 1)] = factor
        st_ref[s, pl.ds(PARTS + 1, 1)] = jnp.sum(factor * st_ref[s, pl.ds(2 * PARTS + 2, PARTS + 1)], axis=0, keepdims=True)

    def backward(s, part, first, n):
        rows = pl.ds(part * WIDE + first, n)
        prob = e_ref[s, rows] * st_ref[s, pl.ds(part, 1)]
        ds = (prob * (dp_ref[s, rows] - st_ref[s, pl.ds(PARTS + 1, 1)])).astype(BF16)
        ds_ref[s, rows] = ds
        return nn(ds, q_v[s]) * SCALE, nn(prob.astype(BF16), do_v[s])

    def prefix_grads(i, first, save):
        @pl.loop(0, NS, unroll=UNROLL)
        def _(s):
            prev = prev_ref[s]
            at = jnp.maximum(prev, 0)
            for k, grad in enumerate(backward(s, i, first, ROWS)):
                run[k, s] = grad + jnp.where(prev >= 0, run[k, at], 0.0)

        @pl.loop(0, NP)
        def _(p):
            last = last_ref[p]
            at = jnp.maximum(last, 0)
            for k in range(2):
                save(k, p, jnp.where(last >= 0, run[k, at], 0.0))

    def sibling_grads(i):
        def save(k, p, total):
            sib_send[i, k, p] = total.astype(BF16)

        prefix_grads(i, ROWS, save)
        send(sib_send.at[i], sib_recv.at[i], back_sem.at[i], sibling)

    def own_grads(i):
        def save(k, p, total):
            own_sum[i, k, p] = total

        prefix_grads(i, 0, save)

    def reduce_ring(i):
        arrived(sib_recv.at[i], back_sem.at[i])
        for side in range(2):
            z = (zh + 1 - side) % 2

            @pl.loop(0, 4)
            def _(p):
                for k in range(2):
                    both = own_sum[i, k, z * 4 + p] + sib_recv[i, k, z * 4 + p].astype(F32)
                    g_ref[i, side, p, k] = both.astype(BF16)
            for j, to in enumerate(ring):
                send(g_ref.at[i, side, (y + to[1]) % 4], y_recv.at[i, side, j], y_sem.at[i, side, j], to)

    def chip_total(i, side, k):
        total = g_ref[i, side, y, k].astype(F32)
        for j in range(3):
            total = total + y_recv[i, side, j, k].astype(F32)
        return total

    def reduce_high(i, side):
        for j in range(3):
            arrived(y_recv.at[i, side, j], y_sem.at[i, side, j])
        for j, to in enumerate((high, far, across)):
            if to[0] != side:
                z_send[i, j] = chip_total(i, side, (kv + to[3]) % 2).astype(BF16)
                send(z_send.at[i, j], z_recv.at[i, j], z_sem.at[i, j], to)

    def query_grads(first, count):
        @pl.loop(first, first + count, unroll=4)
        def _(s):
            p = sp_ref[s]
            keys = jnp.concatenate([block_of(0, part, s) for part in range(PARTS + 1)], axis=0)
            dqt = tn(keys, ds_ref[s]) * SCALE
            for h in range(NH):
                dq_v[s, :, pl.ds(h * HD, HD)] = dqt[:, h * RL:(h + 1) * RL].T.astype(BF16)

    sibling_grads(0)
    own_grads(0)
    reduce_ring(0)

    @pl.loop(0, NS, unroll=4)
    def _(s):
        for k, grad in enumerate(backward(s, PARTS, 0, RL)):
            rg[k, s] = grad
            rg_send[k, s] = grad.astype(BF16)

    send(rg_send.at[1 - kv], rg_recv, rg_sem.at[0], across)
    sibling_grads(1)
    own_grads(1)
    query_grads(0, 4)
    reduce_ring(1)
    query_grads(4, 4)
    reduce_high(0, 0)
    reduce_high(0, 1)
    arrived(rg_recv, rg_sem.at[0])

    @pl.loop(0, NS)
    def _(s):
        dr_ref[s] = (rg[kv, s] + rg_recv[s].astype(F32)).astype(BF16)

    reduce_high(1, 0)
    reduce_high(1, 1)
    for i in range(PARTS):
        total = chip_total(i, 1, kv)
        for j in (2, 1, 0):
            arrived(z_recv.at[i, j], z_sem.at[i, j])
            total = total + z_recv[i, j].astype(F32)
        dp_out[pl.ds(i * ROWS, ROWS)] = total.astype(BF16)
    for copy in flying:
        copy.wait_send()


def finish(*refs):
    sem = refs[-1]
    pairs = list(zip(refs[:3], refs[3:6]))
    copies = [pltpu.make_async_copy(src, dst, sem.at[i]) for i, (src, dst) in enumerate(pairs)]
    for copy in copies:
        copy.start()
    for copy in copies:
        copy.wait()


def shards(queries, resp_kv, prefix_kv, grad_out, lengths, slot_prompt):
    vmem = pl.BlockSpec(memory_space=pltpu.VMEM)
    hbm = pl.BlockSpec(memory_space=pltpu.HBM)
    dma = pltpu.SemaphoreType.DMA
    dq, dr, dp = pl.pallas_call(
        kernel,
        out_shape=[
            pltpu.VMEM((NS, RL, COLS), BF16),
            pltpu.VMEM((NS, RL, HD), BF16),
            pltpu.VMEM((HALF, HD), BF16),
        ],
        in_specs=[hbm, hbm, hbm, hbm, hbm, hbm],
        out_specs=[vmem, vmem, vmem],
        scratch_shapes=[pltpu.VMEM((2, NP, ROWS, HD), BF16)] * (2 * PARTS) + [
            pltpu.VMEM((2, NS, RL, HD), BF16),
            pltpu.VMEM((NS, COLS, HD), BF16),
            pltpu.VMEM((NS, COLS, HD), BF16),
            pltpu.VMEM((NS, PL + RL, COLS), F32),
            pltpu.VMEM((NS, PL + RL, COLS), F32),
            pltpu.VMEM((NS, PL + RL, COLS), BF16),
            pltpu.VMEM((NS, 16, COLS), F32),
            pltpu.VMEM((2, NS, ROWS, HD), F32),
            pltpu.VMEM((PARTS, 2, NP, ROWS, HD), F32),
            pltpu.VMEM((2, NS, RL, HD), F32),
            pltpu.VMEM((2, NS, RL, HD), BF16),
            pltpu.VMEM((NS, RL, HD), BF16),
            pltpu.VMEM((PARTS, 2, NP, ROWS, HD), BF16),
            pltpu.VMEM((PARTS, 2, NP, ROWS, HD), BF16),
            pltpu.VMEM((PARTS, 2, 4, 2, ROWS, HD), BF16),
            pltpu.VMEM((PARTS, 2, 3, 2, ROWS, HD), BF16),
            pltpu.VMEM((PARTS, 3, ROWS, HD), BF16),
            pltpu.VMEM((PARTS, 3, ROWS, HD), BF16),
            pltpu.SMEM((NS,), jnp.int32),
            pltpu.SMEM((NS,), jnp.int32),
            pltpu.SMEM((NS,), jnp.int32),
            pltpu.SMEM((NP,), jnp.int32),
            dma((11 + PARTS,)),
            dma((SENDS,)),
            dma((PARTS, 2, NP)),
            dma((PARTS, 4)),
            dma((PARTS, 2)),
            dma((PARTS,)),
            dma((PARTS, 2, 3)),
            dma((PARTS, 3)),
            dma((1,)),
            dma((1,)),
        ],
        compiler_params=pltpu.CompilerParams(
            collective_id=0, has_side_effects=True, vmem_limit_bytes=62 * 2**20
        ),
    )(
        slot_prompt,
        lengths,
        queries.reshape(NS, RL, COLS),
        grad_out.reshape(NS, RL, COLS),
        resp_kv.reshape(NS, RL, HD),
        prefix_kv,
    )
    return dq.reshape(NS * RL, COLS), dr.reshape(NS * RL, HD), dp


def solution(mesh):
    spec = P("group", "tensor")
    return jax.shard_map(
        shards,
        mesh=mesh,
        in_specs=(spec, spec, spec, spec, P("group"), P("group")),
        out_specs=(spec, spec, spec),
        check_vma=False,
    )
```
